32 devices in a mesh: gx: 4 (over y, x), gy: 8 (over z, core).
Axes of the slice: x: 2, y: 2, z: 4, core: 2. Of those that a mesh axis runs over, the one named last changes fastest.
Arguments:
- pulses_in: float32 [12, 64, 128, 256], P(None, 'gx', 'gy'), may hold values from -6 to 6
- node_loss: float32 [64, 128, 256], P('gx', 'gy'), may hold values from 0.5 to 1
- surface_cells: int32 [4, 8, 512], P('gx', 'gy'), may hold values from 0 to 65535
- surface_normal: int32 [4, 8, 512], P('gx', 'gy'), may hold values from 0 to 6, as said below
- owner_dirs: int32 [4096], replicated, may hold values from 0 to 4095, each once
Outputs:
- pulses_out: float32 [12, 64, 128, 256], P(None, 'gx', 'gy')
- far_field: float32 [4096, 96], P(('gx', 'gy'))
The draws below stay inside these ranges and needn't reach their ends.
Inputs may be any that keep to these rules, and one draw needn't show every extreme that they name: `surface_normal`: on each device the live slots (codes 1 to 6: outward normal +x, -x, +y, -y, +z, -z) come first and the rest are 0; at most 512 are live on a device and some device has all 512 live.
All inputs are finite; a program needn't handle non-finite values.
Results may differ from the reference program's by a relative error of at most 0.0003.
Values sent between devices are 32-bit elements; how exact they have to be, the bound alone decides.
A program may use at most 128 MiB of HBM per device.

```python
import math
import jax
import jax.numpy as jnp
import numpy as np
from jax import lax

CX = 16
CY = 16
CZ = 256
CAP = 512
DIRS = 4096
FREQ = 8
NX = 64
NY = 128
NZ = 256
N_GX = 4
N_GY = 8


def draw_surface_normal(key, part):
    key = jax.random.fold_in(key, 7)
    key_count, key_full, key_code = jax.random.split(key, 3)
    devices_all = N_GX * N_GY
    uniform_count = jax.random.randint(key_count, (devices_all,), 0, CAP + 1)
    live_count = uniform_count * (uniform_count + CAP) // (2 * CAP)
    full_device = jax.random.randint(key_full, (), 0, devices_all)
    live_count = jnp.where(jnp.arange(devices_all) == full_device, CAP, live_count)
    codes = jax.random.randint(key_code, (devices_all, CAP), 1, 7)
    slot_number = jnp.arange(CAP)
    result = jnp.where(slot_number[None, :] < live_count[:, None], codes, 0)
    return result.reshape(N_GX, N_GY, CAP).astype(jnp.int32)


def plant(drawn, key, least, largest):
    index_at = [jax.random.randint(jax.random.fold_in(key, axis), (), 0, length) for axis, length in enumerate(drawn.shape)]
    longest = drawn.shape.index(max(drawn.shape))
    neighbour = index_at[:longest] + [(index_at[longest] + 1) % drawn.shape[longest]] + index_at[longest + 1:]
    return drawn.at[tuple(index_at)].set(least).at[tuple(neighbour)].set(largest)


def block_levels(key, dims, cuts, low, high):
    loudness, own = 1.0, jax.random.fold_in(key, 6)
    for axis_at, blocks in cuts:
        heights = jnp.exp(jax.random.uniform(jax.random.fold_in(own, axis_at), (blocks,), jnp.float32, low / len(cuts), high / len(cuts)))
        loudness = loudness * jnp.repeat(heights, dims[axis_at] // blocks).reshape([-1 if axis == axis_at else 1 for axis in range(len(dims))])
    return loudness


def gaussian(own_key, extent, scale, bound, cuts=(), kind=jnp.bfloat16):
    factor_of = block_levels(own_key, extent, cuts, -0.22, 0.18) if cuts else 1.0
    values = jax.random.normal(own_key, extent, jnp.float32) * scale * factor_of
    return jnp.minimum(jnp.maximum(values, -bound), bound).astype(kind)


def setup_inputs(seed: int = 0) -> dict:
    seeds = jax.random.split(jax.random.key(seed), 6)
    pulses_in = gaussian(seeds[0], (12, NX, NY, NZ), 1.0, 6.0, ((1, 4), (2, 8)), jnp.float32)
    node_loss = jnp.clip(0.5 + 0.5 * jax.random.uniform(seeds[1], (NX, NY, NZ), jnp.float32) ** block_levels(seeds[1], (NX, NY, NZ), ((0, 4), (1, 8)), -0.2, 0.2), 0.5, 1.0)
    surface_cells = plant(jax.random.randint(seeds[2], (N_GX, N_GY, CAP), 0, CX * CY * CZ), jax.random.fold_in(seeds[2], 1), 0, (CX * CY * CZ) - 1).astype(jnp.int32)
    surface_normal = draw_surface_normal(jax.random.fold_in(seeds[5], 71), 0)
    owner_dirs = jax.random.permutation(seeds[4], DIRS).astype(jnp.int32)
    return dict(pulses_in=pulses_in, node_loss=node_loss, surface_cells=surface_cells, surface_normal=surface_normal, owner_dirs=owner_dirs)


HIGH = lax.Precision.HIGHEST
OTHERS = ((1, 2), (0, 2), (0, 1))

def port_of(arm_axis, arm_sign, polarity):
    return 4 * arm_axis + (0 if arm_sign > 0 else 2) + OTHERS[arm_axis].index(polarity)

def node_tables():
    scatter_table = np.zeros((12, 12))
    field_table = np.zeros((6, 12))
    for arm_axis in range(3):
        for arm_sign in (1, -1):
            for polarity in OTHERS[arm_axis]:
                port_k = port_of(arm_axis, arm_sign, polarity)
                third_axis = 3 - arm_axis - polarity
                scatter_table[port_k, port_of(third_axis, 1, polarity)] += 0.5
                scatter_table[port_k, port_of(third_axis, -1, polarity)] += 0.5
                scatter_table[port_k, port_of(polarity, -1, arm_axis)] += 0.5 * arm_sign
                scatter_table[port_k, port_of(polarity, 1, arm_axis)] -= 0.5 * arm_sign
                field_table[polarity, port_k] += 0.5
    for third_axis in range(3):
        first_axis, second_axis = OTHERS[third_axis]
        field_table[3 + third_axis, port_of(first_axis, 1, second_axis)] += 0.5
        field_table[3 + third_axis, port_of(first_axis, -1, second_axis)] -= 0.5
        field_table[3 + third_axis, port_of(second_axis, 1, first_axis)] -= 0.5
        field_table[3 + third_axis, port_of(second_axis, -1, first_axis)] += 0.5
    return (scatter_table.astype(np.float32), field_table.astype(np.float32))

def take_next(pulses, along):
    length = pulses.shape[along]
    kept = lax.slice_in_dim(pulses, 1, length, axis=along)
    return jnp.concatenate([kept, jnp.zeros_like(lax.slice_in_dim(pulses, 0, 1, axis=along))], axis=along)

def take_prev(pulses, along):
    length = pulses.shape[along]
    kept = lax.slice_in_dim(pulses, 0, length - 1, axis=along)
    return jnp.concatenate([jnp.zeros_like(lax.slice_in_dim(pulses, 0, 1, axis=along)), kept], axis=along)

def scatter_node(incident, node_loss):
    scatter_table = jnp.asarray(node_tables()[0])
    return node_loss[None] * jnp.einsum('kl,lxyz->kxyz', scatter_table, incident, precision=HIGH)

def connect_all(reflected):
    return jnp.concatenate([take_next(reflected[2:4], 1), take_prev(reflected[0:2], 1), take_next(reflected[6:8], 2), take_prev(reflected[4:6], 2), take_next(reflected[10:12], 3), take_prev(reflected[8:10], 3)], axis=0)

def cross_three(left, right):
    return jnp.stack([left[1] * right[2] - left[2] * right[1], left[2] * right[0] - left[0] * right[2], left[0] * right[1] - left[1] * right[0]])

def surface_currents(slot_pulses, normal_code):
    field_table = jnp.asarray(node_tables()[1])
    fields = jnp.dot(field_table, slot_pulses, precision=HIGH)
    live = normal_code > 0
    normal_axis = (normal_code - 1) // 2
    outward = 1.0 - 2.0 * ((normal_code - 1) % 2).astype(jnp.float32)
    normal = jnp.stack([jnp.where(live & (normal_axis == which), outward, 0.0) for which in range(3)]).astype(jnp.float32)
    return jnp.concatenate([cross_three(normal, fields[3:6]), -cross_three(normal, fields[0:3])], axis=0)

def unit_vectors(direction_ids):
    theta_count = DIRS // 64
    theta = math.pi * ((direction_ids // 64).astype(jnp.float32) + 0.5) / theta_count
    azimuth = 2.0 * math.pi * (direction_ids % 64).astype(jnp.float32) / 64.0
    return jnp.stack([jnp.sin(theta) * jnp.cos(azimuth), jnp.sin(theta) * jnp.sin(azimuth), jnp.cos(theta)], axis=1)

def far_term(direction_ids, slot_data, positions, scale):
    units = unit_vectors(direction_ids)
    projected = jnp.dot(units, positions, precision=HIGH)
    first = slot_data[0:6]
    second = slot_data[6:12]

    def one_freq(f_index):
        omega = 2.0 * math.pi * (f_index + 1.0) / 64.0
        real_part = first * jnp.cos(omega) + second * jnp.cos(2.0 * omega)
        imag_part = -(first * jnp.sin(omega) + second * jnp.sin(2.0 * omega))
        phase_angle = 2.0 * omega * projected
        upper = jnp.concatenate([real_part, imag_part], axis=0)
        lower = jnp.concatenate([-imag_part, real_part], axis=0)
        return jnp.einsum('nm,cm->nc', jnp.cos(phase_angle), upper, precision=HIGH) + jnp.einsum('nm,cm->nc', jnp.sin(phase_angle), lower, precision=HIGH)
    per_freq = lax.map(one_freq, jnp.arange(FREQ, dtype=jnp.float32))
    rows_here = direction_ids.shape[0]
    return jnp.transpose(per_freq, (1, 0, 2)).reshape(rows_here, FREQ * 12) * scale

def reference(pulses_in, node_loss, surface_cells, surface_normal, owner_dirs):
    incident_one = connect_all(scatter_node(pulses_in, node_loss))
    incident_two = connect_all(scatter_node(incident_one, node_loss))
    device_x = jnp.arange(N_GX, dtype=jnp.int32)[:, None, None]
    device_y = jnp.arange(N_GY, dtype=jnp.int32)[None, :, None]
    x_cell = (device_x * CX + surface_cells // (CY * CZ)).reshape(-1)
    y_cell = (device_y * CY + surface_cells // CZ % CY).reshape(-1)
    z_cell = (surface_cells % CZ).reshape(-1)
    flat_index = ((x_cell * NY + y_cell) * NZ + z_cell).astype(jnp.int32)
    codes = surface_normal.reshape(-1)
    slots_one = jnp.take(incident_one.reshape(12, -1), flat_index, axis=1)
    slots_two = jnp.take(incident_two.reshape(12, -1), flat_index, axis=1)
    slot_data = jnp.concatenate([surface_currents(slots_one, codes), surface_currents(slots_two, codes)], axis=0)
    positions = jnp.stack([x_cell.astype(jnp.float32) - (NX - 1) / 2.0, y_cell.astype(jnp.float32) - (NY - 1) / 2.0, z_cell.astype(jnp.float32) - (NZ - 1) / 2.0])
    scale = 1.0 / math.sqrt(N_GX * N_GY * CAP)
    dir_blocks = owner_dirs.reshape(DIRS // 256, 256)

    def block_term(block_ids):
        return far_term(block_ids, slot_data, positions, scale)
    far_field = lax.map(block_term, dir_blocks).reshape(DIRS, FREQ * 12)
    return (incident_two, far_field)
```

```python
import math

import jax
import jax.numpy as jnp
import numpy as np
from jax import lax
from jax.experimental import pallas as pl
from jax.experimental.pallas import tpu as pltpu
from jax.sharding import PartitionSpec as P

DIRS = 4096
FREQ = 8


HIGH = lax.Precision.HIGHEST
OTHERS = ((1, 2), (0, 2), (0, 1))


def shifted(block, axis, distance):
    devices = range(lax.axis_size(axis))
    route = [(i - distance, i) for i in devices if i - distance in devices]
    return lax.ppermute(block, axis, route)


def port_of(arm_axis, arm_sign, polarity):
    return 4 * arm_axis + (0 if arm_sign > 0 else 2) + OTHERS[arm_axis].index(polarity)


def node_tables():
    scatter_table = np.zeros((12, 12))
    field_table = np.zeros((6, 12))
    for arm_axis in range(3):
        for arm_sign in (1, -1):
            for polarity in OTHERS[arm_axis]:
                port_k = port_of(arm_axis, arm_sign, polarity)
                third_axis = 3 - arm_axis - polarity
                scatter_table[port_k, port_of(third_axis, 1, polarity)] += 0.5
                scatter_table[port_k, port_of(third_axis, -1, polarity)] += 0.5
                scatter_table[port_k, port_of(polarity, -1, arm_axis)] += 0.5 * arm_sign
                scatter_table[port_k, port_of(polarity, 1, arm_axis)] -= 0.5 * arm_sign
                field_table[polarity, port_k] += 0.5
    for third_axis in range(3):
        first_axis, second_axis = OTHERS[third_axis]
        field_table[3 + third_axis, port_of(first_axis, 1, second_axis)] += 0.5
        field_table[3 + third_axis, port_of(first_axis, -1, second_axis)] -= 0.5
        field_table[3 + third_axis, port_of(second_axis, 1, first_axis)] -= 0.5
        field_table[3 + third_axis, port_of(second_axis, -1, first_axis)] += 0.5
    return (scatter_table.astype(np.float32), field_table.astype(np.float32))


def scatter_node(incident, node_loss):
    scatter_table = jnp.asarray(node_tables()[0])
    return node_loss[None] * jnp.einsum("kl,lxyz->kxyz", scatter_table, incident, precision=HIGH)


def connect_tile(reflected):
    zero_plane = jnp.zeros_like(reflected[8:10, :, :, :1])
    plus_z = jnp.concatenate([reflected[10:12, :, :, 1:], zero_plane], axis=3)
    minus_z = jnp.concatenate([zero_plane, reflected[8:10, :, :, :-1]], axis=3)
    from_next_x = shifted(reflected[2:4, :1], "gx", -1)
    from_prev_x = shifted(reflected[0:2, -1:], "gx", 1)
    from_next_y = shifted(reflected[6:8, :, :1], "gy", -1)
    from_prev_y = shifted(reflected[4:6, :, -1:], "gy", 1)
    plus_x = jnp.concatenate([reflected[2:4, 1:], from_next_x], axis=1)
    minus_x = jnp.concatenate([from_prev_x, reflected[0:2, :-1]], axis=1)
    plus_y = jnp.concatenate([reflected[6:8, :, 1:], from_next_y], axis=2)
    minus_y = jnp.concatenate([from_prev_y, reflected[4:6, :, :-1]], axis=2)
    return jnp.concatenate([plus_x, minus_x, plus_y, minus_y, plus_z, minus_z], axis=0)


def cross_three(left, right):
    return jnp.stack(
        [
            left[1] * right[2] - left[2] * right[1],
            left[2] * right[0] - left[0] * right[2],
            left[0] * right[1] - left[1] * right[0],
        ]
    )


def surface_currents(slot_pulses, normal_code):
    field_table = jnp.asarray(node_tables()[1])
    fields = jnp.dot(field_table, slot_pulses, precision=HIGH)
    live = normal_code > 0
    normal_axis = (normal_code - 1) // 2
    outward = 1.0 - 2.0 * ((normal_code - 1) % 2).astype(jnp.float32)
    normal = jnp.stack(
        [jnp.where(live & (normal_axis == which), outward, 0.0) for which in range(3)]
    )
    return jnp.concatenate(
        [cross_three(normal, fields[3:6]), -cross_three(normal, fields[0:3])], axis=0
    )


def trig_coefficients():
    nodes = np.cos(np.pi * (np.arange(64) + 0.5) / 64)
    square = 0.125 * (nodes + 1.0)
    turn = np.sqrt(square)
    cos_fit = np.polynomial.chebyshev.Chebyshev.fit(
        square, np.cos(2 * np.pi * turn), 6, domain=[0.0, 0.25]
    )
    sin_fit = np.polynomial.chebyshev.Chebyshev.fit(
        square, np.sin(2 * np.pi * turn) / turn, 6, domain=[0.0, 0.25]
    )
    to_poly = lambda fit: [float(v) for v in fit.convert(kind=np.polynomial.Polynomial).coef]
    return to_poly(cos_fit), to_poly(sin_fit)


def horner(coefficients, at):
    total = jnp.full_like(at, coefficients[-1])
    for value in coefficients[-2::-1]:
        total = total * at + value
    return total


def cos_sin_turns(turns):
    cos_poly, sin_poly = trig_coefficients()
    rest = turns - jnp.round(turns)
    square = rest * rest
    return horner(cos_poly, square), rest * horner(sin_poly, square)


def split_two(values):
    high = values.astype(jnp.bfloat16)
    low = (values - high.astype(jnp.float32)).astype(jnp.bfloat16)
    return high, low


def output_weights(scale):
    weights = np.zeros((FREQ, 2, 2, 16, FREQ * 12))
    for f in range(FREQ):
        for t in (1, 2):
            w = 2.0 * math.pi * (f + 1) / 64.0 * t
            for c in range(6):
                row = 8 * (t - 1) + c
                weights[f, 0, :, row, 12 * f + c] = math.cos(w)
                weights[f, 1, :, row, 12 * f + c] = math.sin(w)
                weights[f, 0, :, row, 12 * f + 6 + c] = -math.sin(w)
                weights[f, 1, :, row, 12 * f + 6 + c] = math.cos(w)
    return (weights * scale).reshape(2 * FREQ, 32, 12 * FREQ).astype(np.float32)


CHUNK = 256
GROUP = 32


def far_kernel(gathered, dirs, weights, out, packed, totals, counts_v, counts_s, sem):
    devices, _, slots = gathered.shape
    rows = dirs.shape[1]
    flags = gathered[:, 15, :]
    live = jnp.sum(flags, axis=1, keepdims=True).astype(jnp.int32)
    counts_v[...] = jnp.broadcast_to(live, counts_v.shape)
    copy = pltpu.make_async_copy(counts_v, counts_s, sem)
    copy.start()

    ids = dirs[...]
    theta = (ids // 64).astype(jnp.float32) * (1.0 / 128.0) + 1.0 / 256.0
    azimuth = (ids % 64).astype(jnp.float32) * (1.0 / 64.0)
    cos_t, sin_t = cos_sin_turns(theta)
    cos_a, sin_a = cos_sin_turns(azimuth)
    units = jnp.concatenate([sin_t * cos_a, sin_t * sin_a, cos_t], axis=0) * (1.0 / 32.0)
    first = units.astype(jnp.bfloat16).astype(jnp.float32)
    second = (units - first).astype(jnp.bfloat16).astype(jnp.float32)
    third = units - first - second
    stack = jnp.concatenate(
        [first, second, third, first, second, jnp.zeros((rows - 15, rows), jnp.float32)], axis=0
    )
    unit_cols = stack.T[:, :16].astype(jnp.bfloat16)
    totals[...] = jnp.zeros_like(totals)
    copy.wait()

    lane = lax.broadcasted_iota(jnp.int32, (16, 128), 1)
    pad = jnp.zeros((16, 128), jnp.float32)

    def pack(d, offset):
        base = pl.multiple_of((offset >> 7) << 7, 128)
        shift = offset & 127
        block = pltpu.roll(jnp.concatenate([gathered[d], pad], axis=1), shift, 1)
        packed[:, pl.ds(base, 128)] = jnp.where(
            lane < shift, packed[:, pl.ds(base, 128)], block[:, :128]
        )
        packed[:, pl.ds(base + 128, slots)] = block[:, 128:]
        packed[:, pl.ds(base + 128 + slots, CHUNK)] = jnp.zeros((16, CHUNK), jnp.float32)
        return offset + counts_s[d, 0]

    total = lax.fori_loop(0, devices, pack, jnp.int32(0))

    def chunk_step(index, carry):
        block = packed[:, pl.ds(pl.multiple_of(index * CHUNK, CHUNK), CHUNK)]
        high, low = split_two(block)
        currents = jnp.concatenate([high, low], axis=0)
        place = jnp.concatenate([block[6:8], block[14:15]], axis=0)
        place_high = place.astype(jnp.bfloat16).astype(jnp.float32)
        place_low = place - place_high
        places = jnp.concatenate(
            [place_high] * 3 + [place_low] * 2 + [jnp.zeros((1, CHUNK), jnp.float32)], axis=0
        ).astype(jnp.bfloat16)
        turns = jnp.dot(unit_cols, places, preferred_element_type=jnp.float32)
        for g in range(rows // GROUP):
            cos_one, sin_one = cos_sin_turns(turns[g * GROUP : (g + 1) * GROUP])
            double = 2.0 * cos_one
            cos_old, sin_old = jnp.ones_like(cos_one), jnp.zeros_like(sin_one)
            cos_now, sin_now = cos_one, sin_one
            highs, lows = [], []
            for f in range(FREQ):
                for value in (cos_now, sin_now):
                    upper, lower = split_two(value)
                    highs.append(upper)
                    lows.append(lower)
                if f < FREQ - 1:
                    cos_now, cos_old = double * cos_now - cos_old, cos_now
                    sin_now, sin_old = double * sin_now - sin_old, sin_now
            span = 2 * FREQ * GROUP
            both = jnp.concatenate(highs + lows, axis=0)
            product = lax.dot_general(
                both, currents, (((1,), (1,)), ((), ())), preferred_element_type=jnp.float32
            )
            totals[pl.ds(g * span, span), :] += product[:span] + product[span:]
        return carry

    lax.fori_loop(0, (total + CHUNK - 1) >> 8, chunk_step, 0)

    for g in range(rows // GROUP):
        result = jnp.zeros((GROUP, 12 * FREQ), jnp.float32)
        for k in range(2 * FREQ):
            part = totals[pl.ds((g * 2 * FREQ + k) * GROUP, GROUP), :]
            result += jnp.dot(
                part, weights[k], precision=HIGH, preferred_element_type=jnp.float32
            )
        out[pl.ds(g * GROUP, GROUP), :] = result


def far_field_of(gathered, own_dirs, scale):
    devices, _, slots = gathered.shape
    rows = own_dirs.shape[1]
    vmem = pl.BlockSpec(memory_space=pltpu.VMEM)
    return pl.pallas_call(
        far_kernel,
        out_shape=jax.ShapeDtypeStruct((rows, 12 * FREQ), jnp.float32),
        in_specs=[vmem] * 3,
        out_specs=vmem,
        scratch_shapes=[
            pltpu.VMEM((16, devices * slots + 128 + CHUNK), jnp.float32),
            pltpu.VMEM((2 * FREQ * rows, 32), jnp.float32),
            pltpu.VMEM((devices, 128), jnp.int32),
            pltpu.SMEM((devices, 128), jnp.int32),
            pltpu.SemaphoreType.DMA,
        ],
        compiler_params=pltpu.CompilerParams(vmem_limit_bytes=48 * 1024 * 1024),
    )(gathered, own_dirs, jnp.asarray(output_weights(scale)))


def per_device(pulses_in, node_loss, surface_cells, surface_normal, owner_dirs):
    tile_x = pulses_in.shape[1]
    tile_y = pulses_in.shape[2]
    tile_z = pulses_in.shape[3]
    slot_count = surface_cells.shape[2]
    size_x = lax.axis_size("gx")
    size_y = lax.axis_size("gy")
    incident_one = connect_tile(scatter_node(pulses_in, node_loss))
    incident_two = connect_tile(scatter_node(incident_one, node_loss))
    cell_index = surface_cells[0, 0]
    codes = surface_normal[0, 0]
    slots_one = jnp.take(incident_one.reshape(12, -1), cell_index, axis=1)
    slots_two = jnp.take(incident_two.reshape(12, -1), cell_index, axis=1)
    slot_data = jnp.concatenate(
        [surface_currents(slots_one, codes), surface_currents(slots_two, codes)], axis=0
    )
    x_cell = lax.axis_index("gx") * tile_x + cell_index // (tile_y * tile_z)
    y_cell = lax.axis_index("gy") * tile_y + cell_index // tile_z % tile_y
    z_cell = cell_index % tile_z
    positions = jnp.stack(
        [
            x_cell.astype(jnp.float32) - (tile_x * size_x - 1) / 2.0,
            y_cell.astype(jnp.float32) - (tile_y * size_y - 1) / 2.0,
            z_cell.astype(jnp.float32) - (tile_z - 1) / 2.0,
        ]
    )
    scale = 1.0 / math.sqrt(size_x * size_y * slot_count)
    live = (codes > 0).astype(jnp.float32)[None]
    mine = jnp.concatenate(
        [slot_data[0:6], positions[0:2], slot_data[6:12], positions[2:3], live], axis=0
    )
    gathered = lax.all_gather(mine, ("gx", "gy"))
    rows = owner_dirs.shape[0] // (size_x * size_y)
    own = lax.axis_index("gx") * size_y + lax.axis_index("gy")
    own_dirs = lax.dynamic_slice(owner_dirs, (own * rows,), (rows,))[None]
    far_field = far_field_of(gathered, own_dirs, scale)
    return (incident_two, far_field)


def solution(mesh):
    return jax.shard_map(
        per_device,
        mesh=mesh,
        in_specs=(
            P(None, "gx", "gy", None),
            P("gx", "gy", None),
            P("gx", "gy", None),
            P("gx", "gy", None),
            P(),
        ),
        out_specs=(P(None, "gx", "gy", None), P(("gx", "gy"), None)),
        check_vma=False,
    )
```

```python
import functools
import math

import jax
import jax.numpy as jnp
import numpy as np
from jax import lax
from jax.experimental import pallas as pl
from jax.experimental.pallas import tpu as pltpu
from jax.sharding import PartitionSpec as P

DIRS = 4096
FREQ = 8


HIGH = lax.Precision.HIGHEST
OTHERS = ((1, 2), (0, 2), (0, 1))


def sums_and_differences(ports):
    total, change = {}, {}
    for arm in range(3):
        for at, polarity in enumerate(OTHERS[arm]):
            plus, minus = ports[4 * arm + at], ports[4 * arm + 2 + at]
            total[arm, polarity] = plus + minus
            change[arm, polarity] = plus - minus
    return total, change


def reflect(total, change, half_loss):
    reflected = [None] * 12
    for arm in range(3):
        for at, polarity in enumerate(OTHERS[arm]):
            third = 3 - arm - polarity
            even = total[third, polarity]
            odd = change[polarity, arm]
            reflected[4 * arm + at] = half_loss * (even - odd)
            reflected[4 * arm + 2 + at] = half_loss * (even + odd)
    return reflected


def node_fields(total, change):
    electric = [
        0.5 * (total[OTHERS[p][0], p] + total[OTHERS[p][1], p]) for p in range(3)
    ]
    magnetic = [
        0.5 * (change[OTHERS[r][0], OTHERS[r][1]] - change[OTHERS[r][1], OTHERS[r][0]])
        for r in range(3)
    ]
    return electric + magnetic


def tlm_kernel(
    size_x, size_y,
    pulses, loss, cells, codes,
    pulses_out, gat_one, gat_two,
    refl, y_face, y_halo, result, fields, select_z, picked,
    halo_send, halo_recv, send_z, recv_z, send_x, recv_x, send_c, recv_c, out_sem,
):
    tile_x, tile_y, tile_z = loss.shape
    slots = cells.shape[2]
    half_y = size_y // 2
    gx = lax.axis_index("gx")
    gy = lax.axis_index("gy")
    pair, core = gy // 2, gy % 2
    mesh_ids = pl.DeviceIdType.MESH
    arrives = (gx < size_x - 1, gx > 0, gy < size_y - 1, gy > 0)
    leaves = (gx > 0, gx < size_x - 1, gy > 0, gy < size_y - 1)

    barrier = pltpu.get_barrier_semaphore()

    def greet(x, y):
        pl.semaphore_signal(barrier, inc=1, device_id=(x, y), device_id_type=mesh_ids)

    for o in range(1, half_y):
        greet(gx, 2 * ((pair + o) % half_y) + core)
    for o in range(1, size_x):
        greet((gx + o) % size_x, gy)
    greet(gx, 2 * pair + 1 - core)
    other = gy + 2 * core - 1
    has_other = (other >= 0) & (other < size_y)

    @pl.when(has_other)
    def _():
        greet(gx, other)

    pl.semaphore_wait(barrier, half_y + size_x - 1 + has_other.astype(jnp.int32))

    row = lax.broadcasted_iota(jnp.int32, (tile_y, tile_z), 0)
    lane = lax.broadcasted_iota(jnp.int32, (tile_y, tile_z), 1)

    def halo_copy(t, kind):
        if kind == 0:
            source, target = refl.at[t, pl.ds(2, 2), 1], refl.at[t, pl.ds(2, 2), tile_x + 1]
            place = (gx - 1, gy)
        elif kind == 1:
            source, target = refl.at[t, pl.ds(0, 2), tile_x], refl.at[t, pl.ds(0, 2), 0]
            place = (gx + 1, gy)
        else:
            source, target = y_face.at[t, kind - 2], y_halo.at[t, kind - 2]
            place = (gx, gy - 1 if kind == 2 else gy + 1)
        return pltpu.make_async_remote_copy(
            src_ref=source,
            dst_ref=target,
            send_sem=halo_send.at[t, kind],
            recv_sem=halo_recv.at[t, kind],
            device_id=place,
            device_id_type=mesh_ids,
        )

    def send_halos(t):
        for kind in range(4):
            @pl.when(leaves[kind])
            def _():
                halo_copy(t, kind).start()

    def await_halos(t):
        for kind in range(4):
            @pl.when(arrives[kind])
            def _():
                halo_copy(t, kind).wait_recv()

            @pl.when(jnp.logical_not(arrives[kind]))
            def _():
                zeros = jnp.zeros((2, tile_y, tile_z), jnp.float32)
                if kind == 0:
                    refl[t, 2:4, tile_x + 1] = zeros
                elif kind == 1:
                    refl[t, 0:2, 0] = zeros
                else:
                    y_halo[t, kind - 2] = jnp.zeros((2, tile_x, tile_z), jnp.float32)

    def keep_reflected(t, x, reflected):
        for k in range(12):
            refl[t, k, x + 1] = reflected[k]
        for k in range(2):
            y_face[t, 0, k, pl.ds(x, 1), :] = reflected[6 + k][0:1]
            y_face[t, 1, k, pl.ds(x, 1), :] = reflected[4 + k][tile_y - 1 : tile_y]

    def incident_at(t, x):
        ports = [None] * 12
        for k in range(2):
            ports[k] = refl[t, 2 + k, x + 2]
            ports[2 + k] = refl[t, k, x]
            after = y_halo[t, 0, k, pl.ds(x, 1), :]
            before = y_halo[t, 1, k, pl.ds(x, 1), :]
            ports[4 + k] = jnp.where(
                row == tile_y - 1, after, pltpu.roll(refl[t, 6 + k, x + 1], tile_y - 1, 0)
            )
            ports[6 + k] = jnp.where(row == 0, before, pltpu.roll(refl[t, 4 + k, x + 1], 1, 0))
            ports[8 + k] = jnp.where(
                lane == tile_z - 1, 0.0, pltpu.roll(refl[t, 10 + k, x + 1], tile_z - 1, 1)
            )
            ports[10 + k] = jnp.where(lane == 0, 0.0, pltpu.roll(refl[t, 8 + k, x + 1], 1, 1))
        return ports

    def keep_fields(x, total, change):
        for c, value in enumerate(node_fields(total, change)):
            high, low = split_two(value)
            at = pl.ds(pl.multiple_of(x * tile_y, 16), tile_y)
            fields[0, c, at, :] = high
            fields[1, c, at, :] = low

    def first_step(x, carry):
        total, change = sums_and_differences([pulses[k, x] for k in range(12)])
        keep_reflected(0, x, reflect(total, change, 0.5 * loss[x]))
        return carry

    def second_step(x, carry):
        total, change = sums_and_differences(incident_at(0, x))
        keep_fields(x, total, change)
        keep_reflected(1, x, reflect(total, change, 0.5 * loss[x]))
        return carry

    def last_connection(x, carry):
        ports = incident_at(1, x)
        for k in range(12):
            result[k, x] = ports[k]
        total, change = sums_and_differences(ports)
        keep_fields(x, total, change)
        return carry

    cell = cells[0]
    code = codes[0]
    column = cell // tile_z
    depth = cell % tile_z
    live = code > 0
    axis_of = (code - 1) // 2
    outward = 1.0 - 2.0 * ((code - 1) % 2).astype(jnp.float32)
    normal = [jnp.where(live & (axis_of == k), outward, 0.0) for k in range(3)]

    def pick(c, carry):
        chosen = jnp.dot(fields[0, c], select_z[...], preferred_element_type=jnp.float32)
        chosen += jnp.dot(fields[1, c], select_z[...], preferred_element_type=jnp.float32)
        rows_of = lax.broadcasted_iota(jnp.int32, chosen.shape, 0)
        picked[c] = jnp.sum(jnp.where(rows_of == column, chosen, 0.0), axis=0, keepdims=True)
        return carry

    def keep_currents(gat, extra):
        lax.fori_loop(0, 6, pick, 0)
        electric = [picked[c] for c in range(3)]
        magnetic = [picked[3 + c] for c in range(3)]
        rows = []
        for sign, vector in ((1.0, magnetic), (-1.0, electric)):
            for k in range(3):
                a, b = (k + 1) % 3, (k + 2) % 3
                rows.append(sign * (normal[a] * vector[b] - normal[b] * vector[a]))
        gat[gx, core, pair] = jnp.concatenate(rows + extra, axis=0)

    def gather_copies(t, phase):
        gat = (gat_one, gat_two)[t]
        if phase == 0:
            count, block, sends, recvs = half_y, gat.at[gx, core, pair], send_z, recv_z
            place = lambda o: (gx, 2 * ((pair + o) % half_y) + core)
        elif phase == 1:
            count, block, sends, recvs = size_x, gat.at[gx, core], send_x, recv_x
            place = lambda o: ((gx + o) % size_x, gy)
        else:
            count, block, sends, recvs = 2, gat.at[pl.ds(0, size_x), core], send_c, recv_c
            place = lambda o: (gx, 2 * pair + 1 - core)
        return [
            pltpu.make_async_remote_copy(
                src_ref=block,
                dst_ref=block,
                send_sem=sends.at[t, o],
                recv_sem=recvs.at[t, o],
                device_id=place(o),
                device_id_type=mesh_ids,
            )
            for o in range(1, count)
        ]

    def begin(t, phase):
        for copy in gather_copies(t, phase):
            copy.start()

    def finish(t, phase):
        for copy in gather_copies(t, phase):
            copy.wait()

    lax.fori_loop(0, tile_x, first_step, 0)
    send_halos(0)
    depths = lax.broadcasted_iota(jnp.int32, (tile_z, slots), 0)
    select_z[...] = jnp.where(depths == depth, 1.0, 0.0).astype(jnp.bfloat16)
    await_halos(0)
    lax.fori_loop(0, tile_x, second_step, 0)
    send_halos(1)
    x_place = (gx * tile_x + column // tile_y).astype(jnp.float32) - (tile_x * size_x - 1) / 2.0
    y_place = (gy * tile_y + column % tile_y).astype(jnp.float32) - (tile_y * size_y - 1) / 2.0
    keep_currents(gat_one, [x_place, y_place])
    begin(0, 0)
    await_halos(1)
    lax.fori_loop(0, tile_x, last_connection, 0)
    out_copy = pltpu.make_async_copy(result, pulses_out, out_sem)
    out_copy.start()
    finish(0, 0)
    begin(0, 1)
    z_place = depth.astype(jnp.float32) - (tile_z - 1) / 2.0
    keep_currents(gat_two, [z_place, live.astype(jnp.float32)])
    begin(1, 0)
    finish(0, 1)
    begin(0, 2)
    finish(1, 0)
    begin(1, 1)
    finish(0, 2)
    finish(1, 1)
    begin(1, 2)
    for t in range(2):
        for kind in range(4):
            @pl.when(leaves[kind])
            def _():
                halo_copy(t, kind).wait_send()
    out_copy.wait()
    finish(1, 2)


def tlm_and_slots(pulses_in, node_loss, surface_cells, surface_normal):
    size_x, size_y = lax.axis_size("gx"), lax.axis_size("gy")
    tile_x, tile_y, tile_z = node_loss.shape
    slots = surface_cells.shape[2]
    vmem = pl.BlockSpec(memory_space=pltpu.VMEM)
    gat = jax.ShapeDtypeStruct((size_x, 2, size_y // 2, 8, slots), jnp.float32)
    dma = pltpu.SemaphoreType.DMA
    return pl.pallas_call(
        functools.partial(tlm_kernel, size_x, size_y),
        out_shape=(jax.ShapeDtypeStruct(pulses_in.shape, jnp.float32), gat, gat),
        in_specs=[vmem] * 4,
        out_specs=(pl.BlockSpec(memory_space=pl.ANY), vmem, vmem),
        scratch_shapes=[
            pltpu.VMEM((2, 12, tile_x + 2, tile_y, tile_z), jnp.float32),
            pltpu.VMEM((2, 2, 2, tile_x, tile_z), jnp.float32),
            pltpu.VMEM((2, 2, 2, tile_x, tile_z), jnp.float32),
            pltpu.VMEM(pulses_in.shape, jnp.float32),
            pltpu.VMEM((2, 6, tile_x * tile_y, tile_z), jnp.bfloat16),
            pltpu.VMEM((tile_z, slots), jnp.bfloat16),
            pltpu.VMEM((6, 1, slots), jnp.float32),
            dma((2, 4)),
            dma((2, 4)),
            dma((2, size_y // 2)),
            dma((2, size_y // 2)),
            dma((2, size_x)),
            dma((2, size_x)),
            dma((2, 2)),
            dma((2, 2)),
            dma,
        ],
        compiler_params=pltpu.CompilerParams(
            collective_id=0, has_side_effects=True, vmem_limit_bytes=48 * 1024 * 1024
        ),
    )(pulses_in, node_loss, surface_cells, surface_normal)


def trig_coefficients():
    nodes = np.cos(np.pi * (np.arange(64) + 0.5) / 64)
    square = 0.125 * (nodes + 1.0)
    turn = np.sqrt(square)
    cos_fit = np.polynomial.chebyshev.Chebyshev.fit(
        square, np.cos(2 * np.pi * turn), 6, domain=[0.0, 0.25]
    )
    sin_fit = np.polynomial.chebyshev.Chebyshev.fit(
        square, np.sin(2 * np.pi * turn) / turn, 6, domain=[0.0, 0.25]
    )
    to_poly = lambda fit: [float(v) for v in fit.convert(kind=np.polynomial.Polynomial).coef]
    return to_poly(cos_fit), to_poly(sin_fit)


def horner(coefficients, at):
    total = jnp.full_like(at, coefficients[-1])
    for value in coefficients[-2::-1]:
        total = total * at + value
    return total


def cos_sin_turns(turns):
    cos_poly, sin_poly = trig_coefficients()
    rest = turns - jnp.round(turns)
    square = rest * rest
    return horner(cos_poly, square), rest * horner(sin_poly, square)


def split_two(values):
    high = values.astype(jnp.bfloat16)
    low = (values - high.astype(jnp.float32)).astype(jnp.bfloat16)
    return high, low


def output_weights(scale):
    weights = np.zeros((FREQ, 2, 2, 16, FREQ * 12))
    for f in range(FREQ):
        for t in (1, 2):
            w = 2.0 * math.pi * (f + 1) / 64.0 * t
            for c in range(6):
                row = 8 * (t - 1) + c
                weights[f, 0, :, row, 12 * f + c] = math.cos(w)
                weights[f, 1, :, row, 12 * f + c] = math.sin(w)
                weights[f, 0, :, row, 12 * f + 6 + c] = -math.sin(w)
                weights[f, 1, :, row, 12 * f + 6 + c] = math.cos(w)
    return (weights * scale).reshape(2 * FREQ, 32, 12 * FREQ).astype(np.float32)


CHUNK = 256
GROUP = 32


def far_kernel(gat_one, gat_two, dirs, weights, out, packed, totals, counts_v, counts_s, sem):
    devices, _, slots = gat_one.shape
    rows = dirs.shape[1]
    flags = gat_two[:, 7, :]
    live = jnp.sum(flags, axis=1, keepdims=True).astype(jnp.int32)
    counts_v[...] = jnp.broadcast_to(live, counts_v.shape)
    copy = pltpu.make_async_copy(counts_v, counts_s, sem)
    copy.start()

    ids = dirs[...]
    theta = (ids // 64).astype(jnp.float32) * (1.0 / 128.0) + 1.0 / 256.0
    azimuth = (ids % 64).astype(jnp.float32) * (1.0 / 64.0)
    cos_t, sin_t = cos_sin_turns(theta)
    cos_a, sin_a = cos_sin_turns(azimuth)
    units = jnp.concatenate([sin_t * cos_a, sin_t * sin_a, cos_t], axis=0) * (1.0 / 32.0)
    first = units.astype(jnp.bfloat16).astype(jnp.float32)
    second = (units - first).astype(jnp.bfloat16).astype(jnp.float32)
    third = units - first - second
    stack = jnp.concatenate(
        [first, second, third, first, second, jnp.zeros((rows - 15, rows), jnp.float32)], axis=0
    )
    unit_cols = stack.T[:, :16].astype(jnp.bfloat16)
    totals[...] = jnp.zeros_like(totals)
    copy.wait()

    lane = lax.broadcasted_iota(jnp.int32, (16, 128), 1)
    pad = jnp.zeros((16, 128), jnp.float32)

    def pack(d, offset):
        base = pl.multiple_of((offset >> 7) << 7, 128)
        shift = offset & 127
        block = pltpu.roll(jnp.concatenate([jnp.concatenate([gat_one[d], gat_two[d]], axis=0), pad], axis=1), shift, 1)
        packed[:, pl.ds(base, 128)] = jnp.where(
            lane < shift, packed[:, pl.ds(base, 128)], block[:, :128]
        )
        packed[:, pl.ds(base + 128, slots)] = block[:, 128:]
        packed[:, pl.ds(base + 128 + slots, CHUNK)] = jnp.zeros((16, CHUNK), jnp.float32)
        return offset + counts_s[d, 0]

    total = lax.fori_loop(0, devices, pack, jnp.int32(0))

    def chunk_step(index, carry):
        block = packed[:, pl.ds(pl.multiple_of(index * CHUNK, CHUNK), CHUNK)]
        high, low = split_two(block)
        currents = jnp.concatenate([high, low], axis=0)
        place = jnp.concatenate([block[6:8], block[14:15]], axis=0)
        place_high = place.astype(jnp.bfloat16).astype(jnp.float32)
        place_low = place - place_high
        places = jnp.concatenate(
            [place_high] * 3 + [place_low] * 2 + [jnp.zeros((1, CHUNK), jnp.float32)], axis=0
        ).astype(jnp.bfloat16)
        turns = jnp.dot(unit_cols, places, preferred_element_type=jnp.float32)
        for g in range(rows // GROUP):
            cos_one, sin_one = cos_sin_turns(turns[g * GROUP : (g + 1) * GROUP])
            double = 2.0 * cos_one
            cos_old, sin_old = jnp.ones_like(cos_one), jnp.zeros_like(sin_one)
            cos_now, sin_now = cos_one, sin_one
            highs, lows = [], []
            for f in range(FREQ):
                for value in (cos_now, sin_now):
                    upper, lower = split_two(value)
                    highs.append(upper)
                    lows.append(lower)
                if f < FREQ - 1:
                    cos_now, cos_old = double * cos_now - cos_old, cos_now
                    sin_now, sin_old = double * sin_now - sin_old, sin_now
            span = 2 * FREQ * GROUP
            both = jnp.concatenate(highs + lows, axis=0)
            product = lax.dot_general(
                both, currents, (((1,), (1,)), ((), ())), preferred_element_type=jnp.float32
            )
            totals[pl.ds(g * span, span), :] += product[:span] + product[span:]
        return carry

    lax.fori_loop(0, (total + CHUNK - 1) >> 8, chunk_step, 0)

    for g in range(rows // GROUP):
        result = jnp.zeros((GROUP, 12 * FREQ), jnp.float32)
        for k in range(2 * FREQ):
            part = totals[pl.ds((g * 2 * FREQ + k) * GROUP, GROUP), :]
            result += jnp.dot(
                part, weights[k], precision=HIGH, preferred_element_type=jnp.float32
            )
        out[pl.ds(g * GROUP, GROUP), :] = result


def far_field_of(gat_one, gat_two, own_dirs, scale):
    devices, _, slots = gat_one.shape
    rows = own_dirs.shape[1]
    vmem = pl.BlockSpec(memory_space=pltpu.VMEM)
    return pl.pallas_call(
        far_kernel,
        out_shape=jax.ShapeDtypeStruct((rows, 12 * FREQ), jnp.float32),
        in_specs=[vmem] * 4,
        out_specs=vmem,
        scratch_shapes=[
            pltpu.VMEM((16, devices * slots + 128 + CHUNK), jnp.float32),
            pltpu.VMEM((2 * FREQ * rows, 32), jnp.float32),
            pltpu.VMEM((devices, 128), jnp.int32),
            pltpu.SMEM((devices, 128), jnp.int32),
            pltpu.SemaphoreType.DMA,
        ],
        compiler_params=pltpu.CompilerParams(vmem_limit_bytes=48 * 1024 * 1024),
    )(gat_one, gat_two, own_dirs, jnp.asarray(output_weights(scale)))


def per_device(pulses_in, node_loss, surface_cells, surface_normal, owner_dirs):
    slot_count = surface_cells.shape[2]
    size_x = lax.axis_size("gx")
    size_y = lax.axis_size("gy")
    devices = size_x * size_y
    rows = owner_dirs.shape[0] // devices
    own = lax.axis_index("gx") * size_y + lax.axis_index("gy")
    own_dirs = lax.dynamic_slice(owner_dirs, (own * rows,), (rows,))[None]
    pulses_out, gat_one, gat_two = tlm_and_slots(
        pulses_in, node_loss, surface_cells, surface_normal
    )
    far_field = far_field_of(
        gat_one.reshape(devices, 8, slot_count),
        gat_two.reshape(devices, 8, slot_count),
        own_dirs,
        1.0 / math.sqrt(devices * slot_count),
    )
    return (pulses_out, far_field)


def solution(mesh):
    return jax.shard_map(
        per_device,
        mesh=mesh,
        in_specs=(
            P(None, "gx", "gy", None),
            P("gx", "gy", None),
            P("gx", "gy", None),
            P("gx", "gy", None),
            P(),
        ),
        out_specs=(P(None, "gx", "gy", None), P(("gx", "gy"), None)),
        check_vma=False,
    )
```

```python
import functools
import math

import jax
import jax.numpy as jnp
import numpy as np
from jax import lax
from jax.experimental import pallas as pl
from jax.experimental.pallas import tpu as pltpu
from jax.sharding import PartitionSpec as P

DIRS = 4096
FREQ = 8


HIGH = lax.Precision.HIGHEST
OTHERS = ((1, 2), (0, 2), (0, 1))


def sums_and_differences(ports):
    total, change = {}, {}
    for arm in range(3):
        for at, polarity in enumerate(OTHERS[arm]):
            plus, minus = ports[4 * arm + at], ports[4 * arm + 2 + at]
            total[arm, polarity] = plus + minus
            change[arm, polarity] = plus - minus
    return total, change


def reflect(total, change, half_loss):
    reflected = [None] * 12
    for arm in range(3):
        for at, polarity in enumerate(OTHERS[arm]):
            third = 3 - arm - polarity
            even = total[third, polarity]
            odd = change[polarity, arm]
            reflected[4 * arm + at] = half_loss * (even - odd)
            reflected[4 * arm + 2 + at] = half_loss * (even + odd)
    return reflected


def node_fields(total, change):
    electric = [
        0.5 * (total[OTHERS[p][0], p] + total[OTHERS[p][1], p]) for p in range(3)
    ]
    magnetic = [
        0.5 * (change[OTHERS[r][0], OTHERS[r][1]] - change[OTHERS[r][1], OTHERS[r][0]])
        for r in range(3)
    ]
    return electric + magnetic


def tlm_kernel(
    size_x, size_y,
    pulses_hbm, loss_hbm, cells_hbm, codes_hbm,
    pulses_out, gat_one, gat_two,
    refl, y_face, y_halo, result, fields, select_z, picked,
    loss, cells, codes, load_sem,
    halo_send, halo_recv, send_z, recv_z, send_x, recv_x, send_c, recv_c, out_sem,
):
    tile_x, tile_y, tile_z = loss.shape
    slots = cells.shape[2]
    depth_x = tile_x // 4
    plane_loads = []
    for part in range(4):
        at = pl.ds(part * depth_x, depth_x)
        plane_loads.append(
            [
                pltpu.make_async_copy(
                    pulses_hbm.at[:, at], result.at[:, at], load_sem.at[0, part]
                ),
                pltpu.make_async_copy(loss_hbm.at[at], loss.at[at], load_sem.at[1, part]),
            ]
        )
    slot_loads = [
        pltpu.make_async_copy(cells_hbm, cells, load_sem.at[2, 0]),
        pltpu.make_async_copy(codes_hbm, codes, load_sem.at[2, 1]),
    ]
    for copy in sum(plane_loads, []) + slot_loads:
        copy.start()
    half_y = size_y // 2
    gx = lax.axis_index("gx")
    gy = lax.axis_index("gy")
    pair, core = gy // 2, gy % 2
    mesh_ids = pl.DeviceIdType.MESH
    arrives = (gx < size_x - 1, gx > 0, gy < size_y - 1, gy > 0)
    leaves = (gx > 0, gx < size_x - 1, gy > 0, gy < size_y - 1)

    barrier = pltpu.get_barrier_semaphore()

    def greet(x, y):
        pl.semaphore_signal(barrier, inc=1, device_id=(x, y), device_id_type=mesh_ids)

    for o in range(1, half_y):
        greet(gx, 2 * ((pair + o) % half_y) + core)
    for o in range(1, size_x):
        greet((gx + o) % size_x, gy)
    greet(gx, 2 * pair + 1 - core)
    other = gy + 2 * core - 1
    has_other = (other >= 0) & (other < size_y)

    @pl.when(has_other)
    def _():
        greet(gx, other)

    row = lax.broadcasted_iota(jnp.int32, (tile_y, tile_z), 0)
    lane = lax.broadcasted_iota(jnp.int32, (tile_y, tile_z), 1)

    def halo_copy(t, kind):
        if kind == 0:
            source, target = refl.at[t, pl.ds(2, 2), 1], refl.at[t, pl.ds(2, 2), tile_x + 1]
            place = (gx - 1, gy)
        elif kind == 1:
            source, target = refl.at[t, pl.ds(0, 2), tile_x], refl.at[t, pl.ds(0, 2), 0]
            place = (gx + 1, gy)
        else:
            source, target = y_face.at[t, kind - 2], y_halo.at[t, kind - 2]
            place = (gx, gy - 1 if kind == 2 else gy + 1)
        return pltpu.make_async_remote_copy(
            src_ref=source,
            dst_ref=target,
            send_sem=halo_send.at[t, kind],
            recv_sem=halo_recv.at[t, kind],
            device_id=place,
            device_id_type=mesh_ids,
        )

    def send_halos(t):
        for kind in range(4):
            @pl.when(leaves[kind])
            def _():
                halo_copy(t, kind).start()

    def await_halos(t):
        for kind in range(4):
            @pl.when(arrives[kind])
            def _():
                halo_copy(t, kind).wait_recv()

            @pl.when(jnp.logical_not(arrives[kind]))
            def _():
                zeros = jnp.zeros((2, tile_y, tile_z), jnp.float32)
                if kind == 0:
                    refl[t, 2:4, tile_x + 1] = zeros
                elif kind == 1:
                    refl[t, 0:2, 0] = zeros
                else:
                    y_halo[t, kind - 2] = jnp.zeros((2, tile_x, tile_z), jnp.float32)

    def keep_reflected(t, x, reflected):
        for k in range(12):
            refl[t, k, x + 1] = reflected[k]
        for k in range(2):
            y_face[t, 0, k, pl.ds(x, 1), :] = reflected[6 + k][0:1]
            y_face[t, 1, k, pl.ds(x, 1), :] = reflected[4 + k][tile_y - 1 : tile_y]

    def incident_at(t, x):
        ports = [None] * 12
        for k in range(2):
            ports[k] = refl[t, 2 + k, x + 2]
            ports[2 + k] = refl[t, k, x]
            after = y_halo[t, 0, k, pl.ds(x, 1), :]
            before = y_halo[t, 1, k, pl.ds(x, 1), :]
            ports[4 + k] = jnp.where(
                row == tile_y - 1, after, pltpu.roll(refl[t, 6 + k, x + 1], tile_y - 1, 0)
            )
            ports[6 + k] = jnp.where(row == 0, before, pltpu.roll(refl[t, 4 + k, x + 1], 1, 0))
            ports[8 + k] = jnp.where(
                lane == tile_z - 1, 0.0, pltpu.roll(refl[t, 10 + k, x + 1], tile_z - 1, 1)
            )
            ports[10 + k] = jnp.where(lane == 0, 0.0, pltpu.roll(refl[t, 8 + k, x + 1], 1, 1))
        return ports

    def keep_fields(x, total, change):
        for c, value in enumerate(node_fields(total, change)):
            high, low = split_two(value)
            at = pl.ds(pl.multiple_of(x * tile_y, 16), tile_y)
            fields[0, c, at, :] = high
            fields[1, c, at, :] = low

    def first_step(x, carry):
        total, change = sums_and_differences([result[k, x] for k in range(12)])
        keep_reflected(0, x, reflect(total, change, 0.5 * loss[x]))
        return carry

    def second_step(x, carry):
        total, change = sums_and_differences(incident_at(0, x))
        keep_fields(x, total, change)
        keep_reflected(1, x, reflect(total, change, 0.5 * loss[x]))
        return carry

    def last_connection(x, carry):
        ports = incident_at(1, x)
        for k in range(12):
            result[k, x] = ports[k]
        total, change = sums_and_differences(ports)
        keep_fields(x, total, change)
        return carry

    for copy in slot_loads:
        copy.wait()
    cell = cells[0]
    code = codes[0]
    column = cell // tile_z
    depth = cell % tile_z
    live = code > 0
    axis_of = (code - 1) // 2
    outward = 1.0 - 2.0 * ((code - 1) % 2).astype(jnp.float32)
    normal = [jnp.where(live & (axis_of == k), outward, 0.0) for k in range(3)]

    def pick(c, carry):
        chosen = jnp.dot(fields[0, c], select_z[...], preferred_element_type=jnp.float32)
        chosen += jnp.dot(fields[1, c], select_z[...], preferred_element_type=jnp.float32)
        rows_of = lax.broadcasted_iota(jnp.int32, chosen.shape, 0)
        picked[c] = jnp.sum(jnp.where(rows_of == column, chosen, 0.0), axis=0, keepdims=True)
        return carry

    def keep_currents(gat, extra):
        lax.fori_loop(0, 6, pick, 0)
        electric = [picked[c] for c in range(3)]
        magnetic = [picked[3 + c] for c in range(3)]
        rows = []
        for sign, vector in ((1.0, magnetic), (-1.0, electric)):
            for k in range(3):
                a, b = (k + 1) % 3, (k + 2) % 3
                rows.append(sign * (normal[a] * vector[b] - normal[b] * vector[a]))
        gat[gx, core, pair] = jnp.concatenate(rows + extra, axis=0)

    def gather_copies(t, phase):
        gat = (gat_one, gat_two)[t]
        if phase == 0:
            count, block, sends, recvs = half_y, gat.at[gx, core, pair], send_z, recv_z
            place = lambda o: (gx, 2 * ((pair + o) % half_y) + core)
        elif phase == 1:
            count, block, sends, recvs = size_x, gat.at[gx, core], send_x, recv_x
            place = lambda o: ((gx + o) % size_x, gy)
        else:
            count, block, sends, recvs = 2, gat.at[pl.ds(0, size_x), core], send_c, recv_c
            place = lambda o: (gx, 2 * pair + 1 - core)
        return [
            pltpu.make_async_remote_copy(
                src_ref=block,
                dst_ref=block,
                send_sem=sends.at[t, o],
                recv_sem=recvs.at[t, o],
                device_id=place(o),
                device_id_type=mesh_ids,
            )
            for o in range(1, count)
        ]

    def begin(t, phase):
        for copy in gather_copies(t, phase):
            copy.start()

    def finish(t, phase):
        for copy in gather_copies(t, phase):
            copy.wait()

    for part, copy in enumerate(plane_loads):
        for landing in copy:
            landing.wait()
        lax.fori_loop(part * depth_x, (part + 1) * depth_x, first_step, 0)
    pl.semaphore_wait(barrier, half_y + size_x - 1 + has_other.astype(jnp.int32))
    send_halos(0)
    depths = lax.broadcasted_iota(jnp.int32, (tile_z, slots), 0)
    select_z[...] = jnp.where(depths == depth, 1.0, 0.0).astype(jnp.bfloat16)
    await_halos(0)
    lax.fori_loop(0, tile_x, second_step, 0)
    send_halos(1)
    x_place = (gx * tile_x + column // tile_y).astype(jnp.float32) - (tile_x * size_x - 1) / 2.0
    y_place = (gy * tile_y + column % tile_y).astype(jnp.float32) - (tile_y * size_y - 1) / 2.0
    keep_currents(gat_one, [x_place, y_place])
    begin(0, 0)
    await_halos(1)
    lax.fori_loop(0, tile_x, last_connection, 0)
    out_copy = pltpu.make_async_copy(result, pulses_out, out_sem)
    out_copy.start()
    finish(0, 0)
    begin(0, 1)
    z_place = depth.astype(jnp.float32) - (tile_z - 1) / 2.0
    keep_currents(gat_two, [z_place, live.astype(jnp.float32)])
    begin(1, 0)
    finish(0, 1)
    begin(0, 2)
    finish(1, 0)
    begin(1, 1)
    finish(0, 2)
    finish(1, 1)
    begin(1, 2)
    for t in range(2):
        for kind in range(4):
            @pl.when(leaves[kind])
            def _():
                halo_copy(t, kind).wait_send()
    out_copy.wait()
    finish(1, 2)


def tlm_and_slots(pulses_in, node_loss, surface_cells, surface_normal):
    size_x, size_y = lax.axis_size("gx"), lax.axis_size("gy")
    tile_x, tile_y, tile_z = node_loss.shape
    slots = surface_cells.shape[2]
    vmem = pl.BlockSpec(memory_space=pltpu.VMEM)
    gat = jax.ShapeDtypeStruct((size_x, 2, size_y // 2, 8, slots), jnp.float32)
    dma = pltpu.SemaphoreType.DMA
    return pl.pallas_call(
        functools.partial(tlm_kernel, size_x, size_y),
        out_shape=(jax.ShapeDtypeStruct(pulses_in.shape, jnp.float32), gat, gat),
        in_specs=[pl.BlockSpec(memory_space=pltpu.HBM)] * 4,
        out_specs=(pl.BlockSpec(memory_space=pltpu.HBM), vmem, vmem),
        scratch_shapes=[
            pltpu.VMEM((2, 12, tile_x + 2, tile_y, tile_z), jnp.float32),
            pltpu.VMEM((2, 2, 2, tile_x, tile_z), jnp.float32),
            pltpu.VMEM((2, 2, 2, tile_x, tile_z), jnp.float32),
            pltpu.VMEM(pulses_in.shape, jnp.float32),
            pltpu.VMEM((2, 6, tile_x * tile_y, tile_z), jnp.bfloat16),
            pltpu.VMEM((tile_z, slots), jnp.bfloat16),
            pltpu.VMEM((6, 1, slots), jnp.float32),
            pltpu.VMEM(node_loss.shape, jnp.float32),
            pltpu.VMEM(surface_cells.shape, jnp.int32),
            pltpu.VMEM(surface_normal.shape, jnp.int32),
            dma((3, 4)),
            dma((2, 4)),
            dma((2, 4)),
            dma((2, size_y // 2)),
            dma((2, size_y // 2)),
            dma((2, size_x)),
            dma((2, size_x)),
            dma((2, 2)),
            dma((2, 2)),
            dma,
        ],
        compiler_params=pltpu.CompilerParams(
            collective_id=0, has_side_effects=True, vmem_limit_bytes=48 * 1024 * 1024
        ),
    )(pulses_in, node_loss, surface_cells, surface_normal)


def trig_coefficients():
    nodes = np.cos(np.pi * (np.arange(64) + 0.5) / 64)
    square = 0.125 * (nodes + 1.0)
    turn = np.sqrt(square)
    cos_fit = np.polynomial.chebyshev.Chebyshev.fit(
        square, np.cos(2 * np.pi * turn), 6, domain=[0.0, 0.25]
    )
    sin_fit = np.polynomial.chebyshev.Chebyshev.fit(
        square, np.sin(2 * np.pi * turn) / turn, 6, domain=[0.0, 0.25]
    )
    to_poly = lambda fit: [float(v) for v in fit.convert(kind=np.polynomial.Polynomial).coef]
    return to_poly(cos_fit), to_poly(sin_fit)


def horner(coefficients, at):
    total = jnp.full_like(at, coefficients[-1])
    for value in coefficients[-2::-1]:
        total = total * at + value
    return total


def cos_sin_turns(turns):
    cos_poly, sin_poly = trig_coefficients()
    rest = turns - jnp.round(turns)
    square = rest * rest
    return horner(cos_poly, square), rest * horner(sin_poly, square)


def split_two(values):
    high = values.astype(jnp.bfloat16)
    low = (values - high.astype(jnp.float32)).astype(jnp.bfloat16)
    return high, low


def output_weights(scale):
    weights = np.zeros((FREQ, 2, 2, 16, FREQ * 12))
    for f in range(FREQ):
        for t in (1, 2):
            w = 2.0 * math.pi * (f + 1) / 64.0 * t
            for c in range(6):
                row = 8 * (t - 1) + c
                weights[f, 0, :, row, 12 * f + c] = math.cos(w)
                weights[f, 1, :, row, 12 * f + c] = math.sin(w)
                weights[f, 0, :, row, 12 * f + 6 + c] = -math.sin(w)
                weights[f, 1, :, row, 12 * f + 6 + c] = math.cos(w)
    weights = (weights * scale).reshape(2 * FREQ, 32, 12 * FREQ)
    return weights.transpose(0, 2, 1).astype(np.float32)


CHUNK = 512
GROUP = 128


def far_kernel(
    pulses, gat_one, gat_two, dirs, weights, pulses_out, out, packed, totals, counts_v, counts_s, sem, pulse_sem
):
    devices, _, slots = gat_one.shape
    rows = dirs.shape[1]
    pulse_copy = pltpu.make_async_copy(pulses, pulses_out, pulse_sem)
    pulse_copy.start()
    flags = gat_two[:, 7, :]
    live = jnp.sum(flags, axis=1, keepdims=True).astype(jnp.int32)
    counts_v[...] = jnp.broadcast_to(live, counts_v.shape)
    copy = pltpu.make_async_copy(counts_v, counts_s, sem)
    copy.start()

    ids = dirs[...]
    theta = (ids // 64).astype(jnp.float32) * (1.0 / 128.0) + 1.0 / 256.0
    azimuth = (ids % 64).astype(jnp.float32) * (1.0 / 64.0)
    cos_t, sin_t = cos_sin_turns(theta)
    cos_a, sin_a = cos_sin_turns(azimuth)
    units = jnp.concatenate([sin_t * cos_a, sin_t * sin_a, cos_t], axis=0) * (1.0 / 32.0)
    first = units.astype(jnp.bfloat16).astype(jnp.float32)
    second = (units - first).astype(jnp.bfloat16).astype(jnp.float32)
    third = units - first - second
    stack = jnp.concatenate(
        [first, second, third, first, second, jnp.zeros((1, rows), jnp.float32)], axis=0
    )
    unit_rows = stack.astype(jnp.bfloat16)
    totals[...] = jnp.zeros_like(totals)
    copy.wait()

    lane = lax.broadcasted_iota(jnp.int32, (16, 128), 1)
    pad = jnp.zeros((16, 128), jnp.float32)

    def pack(d, offset):
        base = pl.multiple_of((offset >> 7) << 7, 128)
        shift = offset & 127
        block = pltpu.roll(jnp.concatenate([jnp.concatenate([gat_one[d], gat_two[d]], axis=0), pad], axis=1), shift, 1)
        packed[:, pl.ds(base, 128)] = jnp.where(
            lane < shift, packed[:, pl.ds(base, 128)], block[:, :128]
        )
        packed[:, pl.ds(base + 128, slots)] = block[:, 128:]
        packed[:, pl.ds(base + 128 + slots, CHUNK)] = jnp.zeros((16, CHUNK), jnp.float32)
        return offset + counts_s[d, 0]

    total = lax.fori_loop(0, devices, pack, jnp.int32(0))

    def chunk_step(index, carry):
        block = packed[:, pl.ds(pl.multiple_of(index * CHUNK, CHUNK), CHUNK)]
        high, low = split_two(block)
        currents = jnp.concatenate([high, low], axis=0)
        twice = jnp.concatenate([currents, currents], axis=1)
        place = jnp.concatenate([block[6:8], block[14:15]], axis=0)
        place_high = place.astype(jnp.bfloat16).astype(jnp.float32)
        place_low = place - place_high
        places = jnp.concatenate(
            [place_high] * 3 + [place_low] * 2 + [jnp.zeros((1, CHUNK), jnp.float32)], axis=0
        ).astype(jnp.bfloat16)
        turns = lax.dot_general(
            places, unit_rows, (((0,), (0,)), ((), ())), preferred_element_type=jnp.float32
        )
        product = jnp.zeros(totals.shape, jnp.float32)
        for g in range(CHUNK // GROUP):
            cos_one, sin_one = cos_sin_turns(turns[g * GROUP : (g + 1) * GROUP])
            double = 2.0 * cos_one
            cos_old, sin_old = jnp.ones_like(cos_one), jnp.zeros_like(sin_one)
            cos_now, sin_now = cos_one, sin_one
            highs, lows = [], []
            for f in range(FREQ):
                for value in (cos_now, sin_now):
                    upper, lower = split_two(value)
                    highs.append(upper)
                    lows.append(lower)
                if f < FREQ - 1:
                    cos_now, cos_old = double * cos_now - cos_old, cos_now
                    sin_now, sin_old = double * sin_now - sin_old, sin_now
            both = jnp.concatenate(
                [jnp.concatenate(highs, axis=1), jnp.concatenate(lows, axis=1)], axis=0
            )
            own = currents[:, g * GROUP : (g + 1) * GROUP]
            product += jnp.dot(
                jnp.concatenate([own, own], axis=1), both, preferred_element_type=jnp.float32
            )
        totals[...] += product
        return carry

    lax.fori_loop(0, (total + CHUNK - 1) // CHUNK, chunk_step, 0)

    result = jnp.zeros((12 * FREQ, rows), jnp.float32)
    for k in range(2 * FREQ):
        result += jnp.dot(
            weights[k],
            totals[:, k * rows : (k + 1) * rows],
            precision=HIGH,
            preferred_element_type=jnp.float32,
        )
    out[...] = result
    pulse_copy.wait()


def far_field_of(pulses, gat_one, gat_two, own_dirs, scale):
    devices, _, slots = gat_one.shape
    rows = own_dirs.shape[1]
    vmem = pl.BlockSpec(memory_space=pltpu.VMEM)
    return pl.pallas_call(
        far_kernel,
        out_shape=(
            jax.ShapeDtypeStruct(pulses.shape, jnp.float32),
            jax.ShapeDtypeStruct((12 * FREQ, rows), jnp.float32),
        ),
        in_specs=[pl.BlockSpec(memory_space=pltpu.HBM)] + [vmem] * 4,
        out_specs=(pl.BlockSpec(memory_space=pltpu.HBM), vmem),
        scratch_shapes=[
            pltpu.VMEM((16, devices * slots + 128 + CHUNK), jnp.float32),
            pltpu.VMEM((32, 2 * FREQ * rows), jnp.float32),
            pltpu.VMEM((devices, 128), jnp.int32),
            pltpu.SMEM((devices, 128), jnp.int32),
            pltpu.SemaphoreType.DMA,
            pltpu.SemaphoreType.DMA,
        ],
        compiler_params=pltpu.CompilerParams(vmem_limit_bytes=48 * 1024 * 1024),
    )(pulses, gat_one, gat_two, own_dirs, jnp.asarray(output_weights(scale)))


def per_device(pulses_in, node_loss, surface_cells, surface_normal, owner_dirs):
    slot_count = surface_cells.shape[2]
    size_x = lax.axis_size("gx")
    size_y = lax.axis_size("gy")
    devices = size_x * size_y
    rows = owner_dirs.shape[0] // devices
    own = lax.axis_index("gx") * size_y + lax.axis_index("gy")
    own_dirs = lax.dynamic_slice(owner_dirs, (own * rows,), (rows,))[None]
    pulses_out, gat_one, gat_two = tlm_and_slots(
        pulses_in, node_loss, surface_cells, surface_normal
    )
    pulses_out, far_field = far_field_of(
        pulses_out,
        gat_one.reshape(devices, 8, slot_count),
        gat_two.reshape(devices, 8, slot_count),
        own_dirs,
        1.0 / math.sqrt(devices * slot_count),
    )
    return (pulses_out, far_field.T)


def solution(mesh):
    return jax.shard_map(
        per_device,
        mesh=mesh,
        in_specs=(
            P(None, "gx", "gy", None),
            P("gx", "gy", None),
            P("gx", "gy", None),
            P("gx", "gy", None),
            P(),
        ),
        out_specs=(P(None, "gx", "gy", None), P(("gx", "gy"), None)),
        check_vma=False,
    )
```

```python
import functools
import math

import jax
import jax.numpy as jnp
import numpy as np
from jax import lax
from jax.experimental import pallas as pl
from jax.experimental.pallas import tpu as pltpu
from jax.sharding import PartitionSpec as P

DIRS = 4096
FREQ = 8


HIGH = lax.Precision.HIGHEST
OTHERS = ((1, 2), (0, 2), (0, 1))


def sums_and_differences(ports):
    total, change = {}, {}
    for arm in range(3):
        for at, polarity in enumerate(OTHERS[arm]):
            plus, minus = ports[4 * arm + at], ports[4 * arm + 2 + at]
            total[arm, polarity] = plus + minus
            change[arm, polarity] = plus - minus
    return total, change


def reflect(total, change, half_loss):
    reflected = [None] * 12
    for arm in range(3):
        for at, polarity in enumerate(OTHERS[arm]):
            third = 3 - arm - polarity
            even = total[third, polarity]
            odd = change[polarity, arm]
            reflected[4 * arm + at] = half_loss * (even - odd)
            reflected[4 * arm + 2 + at] = half_loss * (even + odd)
    return reflected


def node_fields(total, change):
    electric = [
        0.5 * (total[OTHERS[p][0], p] + total[OTHERS[p][1], p]) for p in range(3)
    ]
    magnetic = [
        0.5 * (change[OTHERS[r][0], OTHERS[r][1]] - change[OTHERS[r][1], OTHERS[r][0]])
        for r in range(3)
    ]
    return electric + magnetic


def tlm_kernel(
    size_x, size_y,
    pulses_hbm, loss_hbm, cells_hbm, codes_hbm,
    pulses_out, gat_one, gat_two,
    refl, y_face, y_halo, result, fields, select_z, picked,
    loss, cells, codes, load_sem,
    halo_send, halo_recv, send_z, recv_z, send_x, recv_x, send_c, recv_c, out_sem,
):
    tile_x, tile_y, tile_z = loss.shape
    slots = cells.shape[2]
    depth_x = tile_x // 4
    plane_loads = []
    for part in range(4):
        at = pl.ds(part * depth_x, depth_x)
        plane_loads.append(
            [
                pltpu.make_async_copy(
                    pulses_hbm.at[:, at], result.at[:, at], load_sem.at[0, part]
                ),
                pltpu.make_async_copy(loss_hbm.at[at], loss.at[at], load_sem.at[1, part]),
            ]
        )
    slot_loads = [
        pltpu.make_async_copy(cells_hbm, cells, load_sem.at[2, 0]),
        pltpu.make_async_copy(codes_hbm, codes, load_sem.at[2, 1]),
    ]
    for copy in sum(plane_loads, []) + slot_loads:
        copy.start()
    half_y = size_y // 2
    gx = lax.axis_index("gx")
    gy = lax.axis_index("gy")
    pair, core = gy // 2, gy % 2
    mesh_ids = pl.DeviceIdType.MESH
    arrives = (gx < size_x - 1, gx > 0, gy < size_y - 1, gy > 0)
    leaves = (gx > 0, gx < size_x - 1, gy > 0, gy < size_y - 1)

    barrier = pltpu.get_barrier_semaphore()

    def greet(x, y):
        pl.semaphore_signal(barrier, inc=1, device_id=(x, y), device_id_type=mesh_ids)

    for o in range(1, half_y):
        greet(gx, 2 * ((pair + o) % half_y) + core)
    for o in range(1, size_x):
        greet((gx + o) % size_x, gy)
    greet(gx, 2 * pair + 1 - core)
    other = gy + 2 * core - 1
    has_other = (other >= 0) & (other < size_y)

    @pl.when(has_other)
    def _():
        greet(gx, other)

    row = lax.broadcasted_iota(jnp.int32, (tile_y, tile_z), 0)
    lane = lax.broadcasted_iota(jnp.int32, (tile_y, tile_z), 1)

    def halo_copy(t, kind):
        if kind == 0:
            source, target = refl.at[t, pl.ds(2, 2), 1], refl.at[t, pl.ds(2, 2), tile_x + 1]
            place = (gx - 1, gy)
        elif kind == 1:
            source, target = refl.at[t, pl.ds(0, 2), tile_x], refl.at[t, pl.ds(0, 2), 0]
            place = (gx + 1, gy)
        else:
            source, target = y_face.at[t, kind - 2], y_halo.at[t, kind - 2]
            place = (gx, gy - 1 if kind == 2 else gy + 1)
        return pltpu.make_async_remote_copy(
            src_ref=source,
            dst_ref=target,
            send_sem=halo_send.at[t, kind],
            recv_sem=halo_recv.at[t, kind],
            device_id=place,
            device_id_type=mesh_ids,
        )

    def send_halos(t):
        for kind in range(4):
            @pl.when(leaves[kind])
            def _():
                halo_copy(t, kind).start()

    def await_halos(t):
        for kind in range(4):
            @pl.when(arrives[kind])
            def _():
                halo_copy(t, kind).wait_recv()

            @pl.when(jnp.logical_not(arrives[kind]))
            def _():
                zeros = jnp.zeros((2, tile_y, tile_z), jnp.float32)
                if kind == 0:
                    refl[t, 2:4, tile_x + 1] = zeros
                elif kind == 1:
                    refl[t, 0:2, 0] = zeros
                else:
                    y_halo[t, kind - 2] = jnp.zeros((2, tile_x, tile_z), jnp.float32)

    def keep_reflected(t, x, reflected):
        for k in range(12):
            refl[t, k, x + 1] = reflected[k]
        for k in range(2):
            y_face[t, 0, k, pl.ds(x, 1), :] = reflected[6 + k][0:1]
            y_face[t, 1, k, pl.ds(x, 1), :] = reflected[4 + k][tile_y - 1 : tile_y]

    def incident_at(t, x):
        ports = [None] * 12
        for k in range(2):
            ports[k] = refl[t, 2 + k, x + 2]
            ports[2 + k] = refl[t, k, x]
            after = y_halo[t, 0, k, pl.ds(x, 1), :]
            before = y_halo[t, 1, k, pl.ds(x, 1), :]
            ports[4 + k] = jnp.where(
                row == tile_y - 1, after, pltpu.roll(refl[t, 6 + k, x + 1], tile_y - 1, 0)
            )
            ports[6 + k] = jnp.where(row == 0, before, pltpu.roll(refl[t, 4 + k, x + 1], 1, 0))
            ports[8 + k] = jnp.where(
                lane == tile_z - 1, 0.0, pltpu.roll(refl[t, 10 + k, x + 1], tile_z - 1, 1)
            )
            ports[10 + k] = jnp.where(lane == 0, 0.0, pltpu.roll(refl[t, 8 + k, x + 1], 1, 1))
        return ports

    def keep_fields(x, total, change):
        for c, value in enumerate(node_fields(total, change)):
            high, low = split_two(value)
            at = pl.ds(pl.multiple_of(x * tile_y, 16), tile_y)
            fields[0, c, at, :] = high
            fields[1, c, at, :] = low

    def first_step(x, carry):
        total, change = sums_and_differences([result[k, x] for k in range(12)])
        keep_reflected(0, x, reflect(total, change, 0.5 * loss[x]))
        return carry

    def second_step(x, carry):
        total, change = sums_and_differences(incident_at(0, x))
        keep_fields(x, total, change)
        keep_reflected(1, x, reflect(total, change, 0.5 * loss[x]))
        return carry

    def last_connection(x, carry):
        ports = incident_at(1, x)
        for k in range(12):
            result[k, x] = ports[k]
        total, change = sums_and_differences(ports)
        keep_fields(x, total, change)
        return carry

    for copy in slot_loads:
        copy.wait()
    cell = cells[0]
    code = codes[0]
    column = cell // tile_z
    depth = cell % tile_z
    live = code > 0
    axis_of = (code - 1) // 2
    outward = 1.0 - 2.0 * ((code - 1) % 2).astype(jnp.float32)
    normal = [jnp.where(live & (axis_of == k), outward, 0.0) for k in range(3)]

    def pick(c, carry):
        chosen = jnp.dot(fields[0, c], select_z[...], preferred_element_type=jnp.float32)
        chosen += jnp.dot(fields[1, c], select_z[...], preferred_element_type=jnp.float32)
        rows_of = lax.broadcasted_iota(jnp.int32, chosen.shape, 0)
        picked[c] = jnp.sum(jnp.where(rows_of == column, chosen, 0.0), axis=0, keepdims=True)
        return carry

    def keep_currents(gat, extra):
        lax.fori_loop(0, 6, pick, 0)
        electric = [picked[c] for c in range(3)]
        magnetic = [picked[3 + c] for c in range(3)]
        rows = []
        for sign, vector in ((1.0, magnetic), (-1.0, electric)):
            for k in range(3):
                a, b = (k + 1) % 3, (k + 2) % 3
                rows.append(sign * (normal[a] * vector[b] - normal[b] * vector[a]))
        gat[gx, core, pair] = jnp.concatenate(rows + extra, axis=0)

    def gather_copies(t, phase):
        gat = (gat_one, gat_two)[t]
        if phase == 0:
            count, block, sends, recvs = half_y, gat.at[gx, core, pair], send_z, recv_z
            place = lambda o: (gx, 2 * ((pair + o) % half_y) + core)
        elif phase == 1:
            count, block, sends, recvs = size_x, gat.at[gx, core], send_x, recv_x
            place = lambda o: ((gx + o) % size_x, gy)
        else:
            count, block, sends, recvs = 2, gat.at[pl.ds(0, size_x), core], send_c, recv_c
            place = lambda o: (gx, 2 * pair + 1 - core)
        return [
            pltpu.make_async_remote_copy(
                src_ref=block,
                dst_ref=block,
                send_sem=sends.at[t, o],
                recv_sem=recvs.at[t, o],
                device_id=place(o),
                device_id_type=mesh_ids,
            )
            for o in range(1, count)
        ]

    def begin(t, phase):
        for copy in gather_copies(t, phase):
            copy.start()

    def finish(t, phase):
        for copy in gather_copies(t, phase):
            copy.wait()

    for part, copy in enumerate(plane_loads):
        for landing in copy:
            landing.wait()
        lax.fori_loop(part * depth_x, (part + 1) * depth_x, first_step, 0, unroll=2)
    pl.semaphore_wait(barrier, half_y + size_x - 1 + has_other.astype(jnp.int32))
    send_halos(0)
    depths = lax.broadcasted_iota(jnp.int32, (tile_z, slots), 0)
    select_z[...] = jnp.where(depths == depth, 1.0, 0.0).astype(jnp.bfloat16)
    await_halos(0)
    lax.fori_loop(0, tile_x, second_step, 0, unroll=2)
    send_halos(1)
    x_place = (gx * tile_x + column // tile_y).astype(jnp.float32) - (tile_x * size_x - 1) / 2.0
    y_place = (gy * tile_y + column % tile_y).astype(jnp.float32) - (tile_y * size_y - 1) / 2.0
    keep_currents(gat_one, [x_place, y_place])
    begin(0, 0)
    await_halos(1)
    lax.fori_loop(0, tile_x, last_connection, 0, unroll=2)
    out_copy = pltpu.make_async_copy(result, pulses_out, out_sem)
    out_copy.start()
    finish(0, 0)
    begin(0, 1)
    z_place = depth.astype(jnp.float32) - (tile_z - 1) / 2.0
    keep_currents(gat_two, [z_place, live.astype(jnp.float32)])
    begin(1, 0)
    finish(0, 1)
    begin(0, 2)
    finish(1, 0)
    begin(1, 1)
    finish(0, 2)
    finish(1, 1)
    begin(1, 2)
    for t in range(2):
        for kind in range(4):
            @pl.when(leaves[kind])
            def _():
                halo_copy(t, kind).wait_send()
    out_copy.wait()
    finish(1, 2)


def tlm_and_slots(pulses_in, node_loss, surface_cells, surface_normal):
    size_x, size_y = lax.axis_size("gx"), lax.axis_size("gy")
    tile_x, tile_y, tile_z = node_loss.shape
    slots = surface_cells.shape[2]
    vmem = pl.BlockSpec(memory_space=pltpu.VMEM)
    gat = jax.ShapeDtypeStruct((size_x, 2, size_y // 2, 8, slots), jnp.float32)
    dma = pltpu.SemaphoreType.DMA
    return pl.pallas_call(
        functools.partial(tlm_kernel, size_x, size_y),
        out_shape=(jax.ShapeDtypeStruct(pulses_in.shape, jnp.float32), gat, gat),
        in_specs=[pl.BlockSpec(memory_space=pltpu.HBM)] * 4,
        out_specs=(pl.BlockSpec(memory_space=pltpu.HBM), vmem, vmem),
        scratch_shapes=[
            pltpu.VMEM((2, 12, tile_x + 2, tile_y, tile_z), jnp.float32),
            pltpu.VMEM((2, 2, 2, tile_x, tile_z), jnp.float32),
            pltpu.VMEM((2, 2, 2, tile_x, tile_z), jnp.float32),
            pltpu.VMEM(pulses_in.shape, jnp.float32),
            pltpu.VMEM((2, 6, tile_x * tile_y, tile_z), jnp.bfloat16),
            pltpu.VMEM((tile_z, slots), jnp.bfloat16),
            pltpu.VMEM((6, 1, slots), jnp.float32),
            pltpu.VMEM(node_loss.shape, jnp.float32),
            pltpu.VMEM(surface_cells.shape, jnp.int32),
            pltpu.VMEM(surface_normal.shape, jnp.int32),
            dma((3, 4)),
            dma((2, 4)),
            dma((2, 4)),
            dma((2, size_y // 2)),
            dma((2, size_y // 2)),
            dma((2, size_x)),
            dma((2, size_x)),
            dma((2, 2)),
            dma((2, 2)),
            dma,
        ],
        compiler_params=pltpu.CompilerParams(
            collective_id=0, has_side_effects=True, vmem_limit_bytes=48 * 1024 * 1024
        ),
    )(pulses_in, node_loss, surface_cells, surface_normal)


def trig_coefficients():
    nodes = np.cos(np.pi * (np.arange(64) + 0.5) / 64)
    square = 0.125 * (nodes + 1.0)
    turn = np.sqrt(square)
    cos_fit = np.polynomial.chebyshev.Chebyshev.fit(
        square, np.cos(2 * np.pi * turn), 6, domain=[0.0, 0.25]
    )
    sin_fit = np.polynomial.chebyshev.Chebyshev.fit(
        square, np.sin(2 * np.pi * turn) / turn, 6, domain=[0.0, 0.25]
    )
    to_poly = lambda fit: [float(v) for v in fit.convert(kind=np.polynomial.Polynomial).coef]
    return to_poly(cos_fit), to_poly(sin_fit)


def horner(coefficients, at):
    total = jnp.full_like(at, coefficients[-1])
    for value in coefficients[-2::-1]:
        total = total * at + value
    return total


def cos_sin_turns(turns):
    cos_poly, sin_poly = trig_coefficients()
    rest = turns - jnp.round(turns)
    square = rest * rest
    return horner(cos_poly, square), rest * horner(sin_poly, square)


def split_two(values):
    high = values.astype(jnp.bfloat16)
    low = (values - high.astype(jnp.float32)).astype(jnp.bfloat16)
    return high, low


def output_weights(scale):
    weights = np.zeros((FREQ, 2, 2, 16, FREQ * 12))
    for f in range(FREQ):
        for t in (1, 2):
            w = 2.0 * math.pi * (f + 1) / 64.0 * t
            for c in range(6):
                row = 8 * (t - 1) + c
                weights[f, 0, :, row, 12 * f + c] = math.cos(w)
                weights[f, 1, :, row, 12 * f + c] = math.sin(w)
                weights[f, 0, :, row, 12 * f + 6 + c] = -math.sin(w)
                weights[f, 1, :, row, 12 * f + 6 + c] = math.cos(w)
    weights = (weights * scale).reshape(2 * FREQ, 32, 12 * FREQ)
    return weights.transpose(0, 2, 1).astype(np.float32)


CHUNK = 512
GROUP = 128


def far_kernel(
    pulses, gat_one, gat_two, dirs, weights, pulses_out, out, packed, totals, counts_v, counts_s, sem, pulse_sem
):
    devices, _, slots = gat_one.shape
    rows = dirs.shape[1]
    pulse_copy = pltpu.make_async_copy(pulses, pulses_out, pulse_sem)
    pulse_copy.start()
    flags = gat_two[:, 7, :]
    live = jnp.sum(flags, axis=1, keepdims=True).astype(jnp.int32)
    counts_v[...] = jnp.broadcast_to(live, counts_v.shape)
    copy = pltpu.make_async_copy(counts_v, counts_s, sem)
    copy.start()

    ids = dirs[...]
    theta = (ids // 64).astype(jnp.float32) * (1.0 / 128.0) + 1.0 / 256.0
    azimuth = (ids % 64).astype(jnp.float32) * (1.0 / 64.0)
    cos_t, sin_t = cos_sin_turns(theta)
    cos_a, sin_a = cos_sin_turns(azimuth)
    units = jnp.concatenate([sin_t * cos_a, sin_t * sin_a, cos_t], axis=0) * (1.0 / 32.0)
    first = units.astype(jnp.bfloat16).astype(jnp.float32)
    second = (units - first).astype(jnp.bfloat16).astype(jnp.float32)
    third = units - first - second
    stack = jnp.concatenate(
        [first, second, third, first, second, jnp.zeros((1, rows), jnp.float32)], axis=0
    )
    unit_rows = stack.astype(jnp.bfloat16)
    totals[...] = jnp.zeros_like(totals)
    copy.wait()

    lane = lax.broadcasted_iota(jnp.int32, (16, 128), 1)
    pad = jnp.zeros((16, 128), jnp.float32)

    def pack(d, offset):
        base = pl.multiple_of((offset >> 7) << 7, 128)
        shift = offset & 127
        block = pltpu.roll(jnp.concatenate([jnp.concatenate([gat_one[d], gat_two[d]], axis=0), pad], axis=1), shift, 1)
        packed[:, pl.ds(base, 128)] = jnp.where(
            lane < shift, packed[:, pl.ds(base, 128)], block[:, :128]
        )
        packed[:, pl.ds(base + 128, slots)] = block[:, 128:]
        packed[:, pl.ds(base + 128 + slots, CHUNK)] = jnp.zeros((16, CHUNK), jnp.float32)
        return offset + counts_s[d, 0]

    total = lax.fori_loop(0, devices, pack, jnp.int32(0))

    def chunk_step(index, carry):
        block = packed[:, pl.ds(pl.multiple_of(index * CHUNK, CHUNK), CHUNK)]
        high, low = split_two(block)
        currents = jnp.concatenate([high, low], axis=0)
        twice = jnp.concatenate([currents, currents], axis=1)
        place = jnp.concatenate([block[6:8], block[14:15]], axis=0)
        place_high = place.astype(jnp.bfloat16).astype(jnp.float32)
        place_low = place - place_high
        places = jnp.concatenate(
            [place_high] * 3 + [place_low] * 2 + [jnp.zeros((1, CHUNK), jnp.float32)], axis=0
        ).astype(jnp.bfloat16)
        turns = lax.dot_general(
            places, unit_rows, (((0,), (0,)), ((), ())), preferred_element_type=jnp.float32
        )
        product = jnp.zeros(totals.shape, jnp.float32)
        for g in range(CHUNK // GROUP):
            cos_one, sin_one = cos_sin_turns(turns[g * GROUP : (g + 1) * GROUP])
            double = 2.0 * cos_one
            cos_old, sin_old = jnp.ones_like(cos_one), jnp.zeros_like(sin_one)
            cos_now, sin_now = cos_one, sin_one
            highs, lows = [], []
            for f in range(FREQ):
                for value in (cos_now, sin_now):
                    upper, lower = split_two(value)
                    highs.append(upper)
                    lows.append(lower)
                if f < FREQ - 1:
                    cos_now, cos_old = double * cos_now - cos_old, cos_now
                    sin_now, sin_old = double * sin_now - sin_old, sin_now
            both = jnp.concatenate(
                [jnp.concatenate(highs, axis=1), jnp.concatenate(lows, axis=1)], axis=0
            )
            own = currents[:, g * GROUP : (g + 1) * GROUP]
            product += jnp.dot(
                jnp.concatenate([own, own], axis=1), both, preferred_element_type=jnp.float32
            )
        totals[...] += product
        return carry

    lax.fori_loop(0, (total + CHUNK - 1) // CHUNK, chunk_step, 0)

    result = jnp.zeros((12 * FREQ, rows), jnp.float32)
    for k in range(2 * FREQ):
        result += jnp.dot(
            weights[k],
            totals[:, k * rows : (k + 1) * rows],
            precision=HIGH,
            preferred_element_type=jnp.float32,
        )
    out[...] = result
    pulse_copy.wait()


def far_field_of(pulses, gat_one, gat_two, own_dirs, scale):
    devices, _, slots = gat_one.shape
    rows = own_dirs.shape[1]
    vmem = pl.BlockSpec(memory_space=pltpu.VMEM)
    return pl.pallas_call(
        far_kernel,
        out_shape=(
            jax.ShapeDtypeStruct(pulses.shape, jnp.float32),
            jax.ShapeDtypeStruct((12 * FREQ, rows), jnp.float32),
        ),
        in_specs=[pl.BlockSpec(memory_space=pltpu.HBM)] + [vmem] * 4,
        out_specs=(pl.BlockSpec(memory_space=pltpu.HBM), vmem),
        scratch_shapes=[
            pltpu.VMEM((16, devices * slots + 128 + CHUNK), jnp.float32),
            pltpu.VMEM((32, 2 * FREQ * rows), jnp.float32),
            pltpu.VMEM((devices, 128), jnp.int32),
            pltpu.SMEM((devices, 128), jnp.int32),
            pltpu.SemaphoreType.DMA,
            pltpu.SemaphoreType.DMA,
        ],
        compiler_params=pltpu.CompilerParams(vmem_limit_bytes=48 * 1024 * 1024),
    )(pulses, gat_one, gat_two, own_dirs, jnp.asarray(output_weights(scale)))


def per_device(pulses_in, node_loss, surface_cells, surface_normal, owner_dirs):
    slot_count = surface_cells.shape[2]
    size_x = lax.axis_size("gx")
    size_y = lax.axis_size("gy")
    devices = size_x * size_y
    rows = owner_dirs.shape[0] // devices
    own = lax.axis_index("gx") * size_y + lax.axis_index("gy")
    own_dirs = lax.dynamic_slice(owner_dirs, (own * rows,), (rows,))[None]
    pulses_out, gat_one, gat_two = tlm_and_slots(
        pulses_in, node_loss, surface_cells, surface_normal
    )
    pulses_out, far_field = far_field_of(
        pulses_out,
        gat_one.reshape(devices, 8, slot_count),
        gat_two.reshape(devices, 8, slot_count),
        own_dirs,
        1.0 / math.sqrt(devices * slot_count),
    )
    return (pulses_out, far_field.T)


def solution(mesh):
    return jax.shard_map(
        per_device,
        mesh=mesh,
        in_specs=(
            P(None, "gx", "gy", None),
            P("gx", "gy", None),
            P("gx", "gy", None),
            P("gx", "gy", None),
            P(),
        ),
        out_specs=(P(None, "gx", "gy", None), P(("gx", "gy"), None)),
        check_vma=False,
    )
```
